256 devices in a mesh: expert: 32 (over z, y), dp: 8 (over x, core).
Axes of the slice: x: 4, y: 4, z: 8, core: 2. Of those that a mesh axis runs over, the one named last changes fastest.
Arguments:
- partial_grads: bfloat16 [8, 256, 2, 16, 7168], P('dp', 'expert'), may hold values from -6 to 6
- replica_grads: bfloat16 [8, 64, 16, 7168], P('dp', 'expert'), may hold values from -6 to 6
- replica_item: int32 [64], P('expert'), may hold values from 0 to 511
- weight: float32 [256, 2, 16, 7168], P('expert', None, None, 'dp'), may hold values from -0.125 to 0.125
- first_moment: float32 [256, 2, 16, 7168], P('expert', None, None, 'dp'), may hold values from -3 to 3
- second_moment: float32 [256, 2, 16, 7168], P('expert', None, None, 'dp'), may hold values from 0.05 to 5
- new_position: int32 [256, 2], P('expert'), may hold values from 0 to 511, as said below
Outputs:
- new_weight: float32 [256, 2, 16, 7168], P('expert', None, None, 'dp')
- new_first: float32 [256, 2, 16, 7168], P('expert', None, None, 'dp')
- new_second: float32 [256, 2, 16, 7168], P('expert', None, None, 'dp')
The draws below stay inside these ranges and needn't reach their ends.
Inputs may be any that keep to these rules, and one draw needn't show every extreme that they name: new_position is a permutation of the 512 items; the items of one index of expert that go to any one index of expert (itself included) number at most 1, and exactly 1 for some pairs.
All inputs are finite; a program needn't handle non-finite values.
Results may differ from the reference program's by a relative error of at most 0.0003.
Values sent between devices are 32-bit elements; how exact they have to be, the bound alone decides.
A program may use at most 128 MiB of HBM per device.

```python
import math
import jax
import jax.numpy as jnp
import numpy as np
from jax import lax

D = 7168
FF = 2048
EXP_DEV = 8
LAYERS = 2
ROWS = 16
STEP = 10
EXPERTS = 256
REPLICAS = 64
N_DP = 8


def draw_new_position(key, part):
    key = jax.random.fold_in(key, 7)
    device_count = EXPERTS // EXP_DEV
    per_device = EXP_DEV * LAYERS
    key_order, key_offset, key_slots = jax.random.split(key, 3)
    ordering = jax.random.permutation(key_order, device_count)
    inverse = jnp.argsort(ordering)
    offsets = jax.random.permutation(key_offset, device_count)
    copies = (per_device + device_count - 1) // device_count
    offsets = jnp.tile(offsets, copies)[:per_device]
    sources = jnp.arange(device_count)
    targets = ordering[(inverse[sources][:, None] + offsets[None, :]) % device_count]
    slot_keys = jax.random.split(key_slots, device_count)
    shuffles = jax.vmap(lambda sub_key: jax.random.permutation(sub_key, per_device))(slot_keys)
    columns_idx = jnp.broadcast_to(jnp.arange(per_device)[None, :], (device_count, per_device))
    slot_index = shuffles[targets, columns_idx]
    positions = targets * per_device + slot_index
    return positions.reshape(EXPERTS, LAYERS).astype(jnp.int32)


def plant(entries, own_key, smallest, largest):
    longest = entries.shape.index(max(entries.shape))
    spots = []
    for shift in (0, 1):
        where = [jax.random.randint(jax.random.fold_in(own_key, axis), (), 0, length) for axis, length in enumerate(entries.shape)]
        where[longest] = (where[longest] + shift) % entries.shape[longest]
        spots.append(tuple(where))
    return entries.at[spots[0]].set(smallest).at[spots[1]].set(largest)


def level_of(own_key, dims, cuts, smallest, top_value):
    loudness, own = 1.0, jax.random.fold_in(own_key, 6)
    for axis_at, blocks in cuts:
        steps = jnp.exp(jax.random.uniform(jax.random.fold_in(own, axis_at), (blocks,), jnp.float32, smallest / len(cuts), top_value / len(cuts)))
        loudness = loudness * jnp.repeat(steps, dims[axis_at] // blocks).reshape([-1 if axis == axis_at else 1 for axis in range(len(dims))])
    return loudness


def rank_bounds(amount, skew):
    loads = [(1 << 20) // math.isqrt(rank ** skew) + 1 for rank in range(1, amount + 1)]
    spread = 1 + sum(loads) // (1 << 30)
    return np.cumsum(np.array([max(1, weight // spread) for weight in loads]))


def ranked_ids(key, shape, count, skew):
    listing = rank_bounds(count, skew)
    lot = jax.random.randint(jax.random.fold_in(key, 1), shape, 0, int(listing[count - 1]))
    grade = jnp.searchsorted(jnp.asarray(listing, jnp.int32), lot, side="right")
    return jax.random.permutation(jax.random.fold_in(key, 2), count)[grade].astype(jnp.int32)


def scatter_about(own_key, dims, scale, bound, pieces=(), kind=jnp.bfloat16):
    loudness = level_of(own_key, dims, pieces, -0.22, 0.18) if pieces else 1.0
    entries = jax.random.normal(own_key, dims, jnp.float32) * scale * loudness
    return jnp.minimum(jnp.maximum(entries, -bound), bound).astype(kind)


def setup_inputs(seed: int = 0) -> dict:
    key_list = jax.random.split(jax.random.key(seed), 8)
    return {
        "partial_grads": scatter_about(key_list[0], (N_DP, EXPERTS, LAYERS, ROWS, D), 1.0, 6.0, ((0, 8), (1, 32))),
        "replica_grads": scatter_about(key_list[1], (N_DP, REPLICAS, ROWS, D), 1.0, 6.0, ((0, 8), (1, 32))),
        "replica_item": plant(ranked_ids(key_list[2], (REPLICAS,), EXPERTS * LAYERS, 2), jax.random.fold_in(key_list[2], 3), 0, (EXPERTS * LAYERS) - 1).astype(jnp.int32),
        "weight": scatter_about(key_list[3], (EXPERTS, LAYERS, ROWS, D), FF ** -0.5, 0.125, ((0, 32), (3, 8)), jnp.float32),
        "first_moment": scatter_about(key_list[4], (EXPERTS, LAYERS, ROWS, D), 0.2, 3.0, ((0, 32), (3, 8)), jnp.float32),
        "second_moment": jnp.clip(jnp.exp(math.log(5.0) - 4.6051702 * jax.random.uniform(key_list[5], (EXPERTS, LAYERS, ROWS, D), jnp.float32) ** level_of(key_list[5], (EXPERTS, LAYERS, ROWS, D), ((0, 32), (3, 8)), -0.2, 0.2)), 0.05, 5.0),
        "new_position": draw_new_position(jax.random.fold_in(key_list[7], 71), 0),
    }


beta_one = 0.9
beta_two = 0.95
learn_rate = 0.003
decay_rate = 0.1
epsilon = 1e-08

def adam_update(weight, first_mom, second_mom, gradient):
    first_new = beta_one * first_mom + (1.0 - beta_one) * gradient
    second_new = beta_two * second_mom + (1.0 - beta_two) * gradient * gradient
    first_hat = first_new / (1.0 - beta_one ** STEP)
    second_hat = second_new / (1.0 - beta_two ** STEP)
    weight_new = weight - learn_rate * (first_hat / (jnp.sqrt(second_hat) + epsilon) + decay_rate * weight)
    return (weight_new, first_new, second_new)

def reference(partial_grads, replica_grads, replica_item, weight, first_moment, second_moment, new_position):
    item_count = EXPERTS * LAYERS
    summed = lax.optimization_barrier(jnp.sum(partial_grads, axis=0, dtype=jnp.float32)).reshape(item_count, ROWS, D)
    replica_sum = lax.optimization_barrier(jnp.sum(replica_grads, axis=0, dtype=jnp.float32))
    gradient = summed.at[replica_item.astype(jnp.int32)].add(replica_sum)
    updated, first_new, second_new = adam_update(weight.reshape(item_count, ROWS, D), first_moment.reshape(item_count, ROWS, D), second_moment.reshape(item_count, ROWS, D), gradient)
    target_pos = new_position.reshape(item_count).astype(jnp.int32)

    def placed(values):
        return jnp.zeros_like(values).at[target_pos].set(values).reshape(EXPERTS, LAYERS, ROWS, D)
    return (placed(updated), placed(first_new), placed(second_new))
```

```python
import functools

import jax
import jax.numpy as jnp
from jax import lax
from jax.experimental import pallas as pl
from jax.experimental.pallas import tpu as pltpu
from jax.sharding import PartitionSpec as P

STEP = 10

beta_one = 0.9
beta_two = 0.95
learn_rate = 0.003
decay_rate = 0.1
epsilon = 1e-08

MESH = pl.DeviceIdType.MESH
NZ, NY, NX = 8, 4, 4
NE = NZ * NY
ITEMS = 16
CHUNKS = 9
R, C = 16, 896

ORDER = [dz * NY + dy for dz in (1, 7, 2, 6, 3, 5, 4, 0) for dy in (0, 1, 3, 2) if (dz, dy) != (0, 0)]


def kernel(
    pos_s, rit_s, rg_h, pg_h, w_h, m_h, v_h,
    ow, om, ov,
    gr, w_v, m_v, v_v, cs, cr, ra, rb, sm, ag, ch, sw, smv, rw, rmv,
    info, infos, tab, inv_s, tab_s,
    ld, tabsem, core_ss, core_rs, a_ss, a_rs, b_ss, b_rs,
    i_ss, i_rs, w_ss, w_rs, mv_ss, mv_rs, gz_ss, gz_rs, gy_ss, gy_rs, gf_ss, gf_rs,
):
    e = lax.axis_index("expert")
    d = lax.axis_index("dp")
    z, y = e // NY, e % NY
    x, c = d // 2, d % 2
    x_next, x_prev, x_far = (x + 1) % NX, (x + 3) % NX, (x + 2) % NX

    def holder(q):
        return ((z + q // NY) % NZ) * NY + (y + q % NY) % NY

    def at_expert(index):
        return (index, d)

    def at_x(index):
        return (e, index * 2 + c)

    other_core = (e, x * 2 + 1 - c)

    loads = [
        pltpu.make_async_copy(rg_h, gr.at[pl.ds(0, 2)], ld.at[0]),
        pltpu.make_async_copy(w_h, w_v, ld.at[9]),
        *[
            pltpu.make_async_copy(pg_h.at[pl.ds(2 * i - 2, 2)], gr.at[pl.ds(2 * i, 2)], ld.at[i])
            for i in range(1, CHUNKS)
        ],
        pltpu.make_async_copy(m_h, m_v, ld.at[10]),
        pltpu.make_async_copy(v_h, v_v, ld.at[11]),
    ]
    for load in loads:
        load.start()
    gr_loads = [loads[0]] + loads[2:10]

    sub = lax.broadcasted_iota(jnp.int32, (8, 128), 0)
    lane = lax.broadcasted_iota(jnp.int32, (8, 128), 1)
    tile = jnp.where(sub == 0, -1, 0)
    for j in range(ITEMS):
        place = pos_s[j // 2, j % 2]
        hit = lane == place // ITEMS
        tile = jnp.where(hit & (sub == 0), place % ITEMS, tile)
        tile = jnp.where(hit & (sub == 2), j, tile)
    for k in range(2):
        tile = jnp.where((sub == 1) & (lane == k), rit_s[k], tile)
    info[...] = tile
    infos[0] = tile
    inv_copy = pltpu.make_async_copy(info, inv_s, tabsem.at[0])
    inv_copy.start()

    barrier = pltpu.get_barrier_semaphore()
    for q in ORDER:
        pl.semaphore_signal(barrier, inc=1, device_id=at_expert(holder(q)), device_id_type=MESH)
    for peer in (other_core, at_x(x_next), at_x(x_prev)):
        pl.semaphore_signal(barrier, inc=1, device_id=peer, device_id_type=MESH)
    pl.semaphore_wait(barrier, NE - 1 + 3)

    sends = []

    def send(src, dst, ss, rs, peer):
        copy = pltpu.make_async_remote_copy(
            src_ref=src, dst_ref=dst, send_sem=ss, recv_sem=rs, device_id=peer, device_id_type=MESH
        )
        copy.start()
        sends.append(copy)
        return copy

    core_copy, a_copy, b_copy = {}, {}, {}

    def stage_core(i):
        gr_loads[i].wait()
        for xd in range(NX):
            columns = pl.ds(pl.multiple_of((xd * 2 + 1 - c) * C, 128), C)
            for u in range(2):
                cs[i, xd, u] = gr[2 * i + u, :, columns].astype(jnp.float32)
        core_copy[i] = send(cs.at[i], cr.at[i], core_ss.at[i], core_rs.at[i], other_core)

    def stage_a(i):
        core_copy[i].wait_recv()
        for xd in range(NX):
            columns = pl.ds(pl.multiple_of((xd * 2 + c) * C, 128), C)
            for u in range(2):
                cr[i, xd, u] = cr[i, xd, u] + gr[2 * i + u, :, columns].astype(jnp.float32)
        a_copy[i] = (
            send(cr.at[i, x_far, 0], ra.at[i, 0], a_ss.at[i, 0], a_rs.at[i, 0], at_x(x_next)),
            send(cr.at[i, x_far, 1], ra.at[i, 1], a_ss.at[i, 1], a_rs.at[i, 1], at_x(x_prev)),
        )

    def stage_b(i):
        a_copy[i][0].wait_recv()
        cr[i, x_next, 0] = cr[i, x_next, 0] + ra[i, 0]
        a_copy[i][1].wait_recv()
        cr[i, x_prev, 1] = cr[i, x_prev, 1] + ra[i, 1]
        b_copy[i] = (
            send(cr.at[i, x_next], rb.at[i, 0], b_ss.at[i, 0], b_rs.at[i, 0], at_x(x_next)),
            send(cr.at[i, x_prev], rb.at[i, 1], b_ss.at[i, 1], b_rs.at[i, 1], at_x(x_prev)),
        )

    def stage_sum(i):
        b_copy[i][0].wait_recv()
        b_copy[i][1].wait_recv()
        for u in range(2):
            total = cr[i, x, u] + rb[i, 0, u] + rb[i, 1, u]
            if i == 0:
                ag[0, 0, u] = total
            else:
                sm[2 * i - 2 + u] = total

    w_copy = {}

    def send_w(q):
        to = holder(q)
        sw[q] = w_v[inv_s[2, to]]
        w_copy[q] = send(sw.at[q], rw.at[q], w_ss.at[q], w_rs.at[q], at_expert(to))

    w_left = list(ORDER)

    def send_some_w(count):
        for _ in range(min(count, len(w_left))):
            send_w(w_left.pop(0))

    gz_copy, gy_copy, gf_copy = {}, {}, {}

    def gather_z():
        for dz in (4, 3, 5, 2, 6, 1, 7):
            gz_copy[dz] = send(ag.at[0, 0], ag.at[0, dz], gz_ss.at[dz], gz_rs.at[dz], at_expert(holder(dz * NY)))

    def gather_y(dz):
        if dz:
            gz_copy[dz].wait_recv()
        gy_copy[dz] = (
            send(ag.at[0, dz], ag.at[1, dz], gy_ss.at[dz, 0], gy_rs.at[dz, 0], at_expert(holder(1))),
            send(ag.at[0, dz], ag.at[3, dz], gy_ss.at[dz, 1], gy_rs.at[dz, 1], at_expert(holder(3))),
        )

    def forward_y(dz):
        gy_copy[dz][0].wait_recv()
        gy_copy[dz][1].wait_recv()
        if dz % 2:
            gf_copy[dz] = send(ag.at[1, dz], ag.at[2, dz], gf_ss.at[dz], gf_rs.at[dz], at_expert(holder(1)))
        else:
            gf_copy[dz] = send(ag.at[3, dz], ag.at[2, dz], gf_ss.at[dz], gf_rs.at[dz], at_expert(holder(3)))

    stage_core(0)
    stage_core(1)
    i_copy = {}
    for q in ORDER:
        i_copy[q] = send(info, infos.at[q], i_ss.at[q], i_rs.at[q], at_expert(holder(q)))
    stage_a(0)
    loads[1].wait()
    inv_copy.wait()
    send_some_w(4)
    stage_b(0)
    stage_core(2)
    stage_a(1)
    send_some_w(4)
    stage_b(1)
    stage_core(3)
    stage_a(2)
    stage_sum(0)
    gather_z()
    gather_y(0)
    for i in range(2, CHUNKS):
        send_some_w(4)
        stage_b(i)
        if i + 2 < CHUNKS:
            stage_core(i + 2)
        if i + 1 < CHUNKS:
            stage_a(i + 1)
        stage_sum(i - 1)
        if i == 5:
            for dz in (1, 7, 2, 6, 3, 5, 4):
                gather_y(dz)
    send_some_w(NE)
    stage_sum(CHUNKS - 1)
    for dz in (0, 1, 7, 2, 6, 3, 5, 4):
        forward_y(dz)

    for q in ORDER:
        i_copy[q].wait_recv()
    sub = lax.broadcasted_iota(jnp.int32, (NE, 128), 0)
    lane = lax.broadcasted_iota(jnp.int32, (NE, 128), 1)
    places = jnp.sum(jnp.where(lane == e, infos[:, 0, :], 0), axis=1, keepdims=True)
    tab[0:1, :] = jnp.max(jnp.where(places == lane, sub, 0), axis=0, keepdims=True)
    served = infos[:, 1, :]
    first_slot = jnp.sum(jnp.where(lane == 0, served, 0), axis=1, keepdims=True)
    second_slot = jnp.sum(jnp.where(lane == 1, served, 0), axis=1, keepdims=True)
    column = jnp.concatenate([first_slot, second_slot], axis=0)
    sub = lax.broadcasted_iota(jnp.int32, (2 * NE, 128), 0)
    lane = lax.broadcasted_iota(jnp.int32, (2 * NE, 128), 1)
    row = jnp.sum(jnp.where(sub == lane, column, 0), axis=0, keepdims=True)
    tab[1:2, :] = jnp.max(jnp.where((column == row) & (sub < lane), sub + 1, 0), axis=0, keepdims=True)
    tab[2:3, :] = jnp.max(jnp.where(column == lane + e * ITEMS, sub + 1, 0), axis=0, keepdims=True)
    tab[3:8, :] = jnp.zeros((5, 128), jnp.int32)
    tab_copy = pltpu.make_async_copy(tab, tab_s, tabsem.at[1])
    tab_copy.start()
    loads[10].wait()
    loads[11].wait()
    tab_copy.wait()
    for dz in range(NZ):
        gf_copy[dz].wait_recv()

    ch[0] = jnp.zeros((R, C), jnp.float32)
    for r in range(2 * NE):
        k, q = r // NE, r % NE
        ch[r + 1] = ag[q % NY, q // NY, k] + ch[tab_s[1, r]]

    def moments(q, to, dst):
        j = inv_s[2, to]
        gradient = sm[j] + ch[tab_s[2, j]]
        dst[q, 0] = beta_one * m_v[j] + (1.0 - beta_one) * gradient
        dst[q, 1] = beta_two * v_v[j] + (1.0 - beta_two) * gradient * gradient

    mv_copy = {}
    for q in ORDER:
        to = holder(q)
        moments(q, to, smv)
        mv_copy[q] = send(smv.at[q], rmv.at[q], mv_ss.at[q], mv_rs.at[q], at_expert(to))
    moments(0, e, rmv)
    rw[0] = w_v[inv_s[2, e]]

    for q in ORDER:
        w_copy[q].wait_recv()
    for q in ORDER:
        mv_copy[q].wait_recv()
    for p in range(ITEMS):
        q = tab_s[0, p]
        first, second, weight = rmv[q, 0], rmv[q, 1], rw[q]
        om[p] = first
        ov[p] = second
        first_hat = first / (1.0 - beta_one**STEP)
        second_hat = second / (1.0 - beta_two**STEP)
        ow[p] = weight - learn_rate * (
            first_hat / (jnp.sqrt(second_hat) + epsilon) + decay_rate * weight
        )
    for copy in sends:
        copy.wait_send()


def per_device(
    partial_grads, replica_grads, replica_item, weight, first_moment, second_moment, new_position
):
    f32, i32, bf16 = jnp.float32, jnp.int32, jnp.bfloat16
    vmem, smem, dma = pltpu.VMEM, pltpu.SMEM, pltpu.SemaphoreType.DMA
    slab = (R, C)
    anywhere = pl.BlockSpec(memory_space=pl.ANY)
    in_smem = pl.BlockSpec(memory_space=pltpu.SMEM)
    in_vmem = pl.BlockSpec(memory_space=pltpu.VMEM)
    outs = pl.pallas_call(
        kernel,
        out_shape=[jax.ShapeDtypeStruct((ITEMS, *slab), f32)] * 3,
        in_specs=[in_smem, in_smem] + [anywhere] * 5,
        out_specs=[in_vmem] * 3,
        scratch_shapes=[
            vmem((2 * CHUNKS, R, 8 * C), bf16),
            vmem((ITEMS, *slab), f32),
            vmem((ITEMS, *slab), f32),
            vmem((ITEMS, *slab), f32),
            vmem((CHUNKS, NX, 2, *slab), f32),
            vmem((CHUNKS, NX, 2, *slab), f32),
            vmem((CHUNKS, 2, *slab), f32),
            vmem((CHUNKS, 2, 2, *slab), f32),
            vmem((ITEMS, *slab), f32),
            vmem((NY, NZ, 2, *slab), f32),
            vmem((2 * NE + 1, *slab), f32),
            vmem((NE, *slab), f32),
            vmem((NE, 2, *slab), f32),
            vmem((NE, *slab), f32),
            vmem((NE, 2, *slab), f32),
            vmem((8, 128), i32),
            vmem((NE, 8, 128), i32),
            vmem((8, 128), i32),
            smem((8, 128), i32),
            smem((8, 128), i32),
            dma((12,)),
            dma((2,)),
            dma((CHUNKS,)), dma((CHUNKS,)),
            dma((CHUNKS, 2)), dma((CHUNKS, 2)),
            dma((CHUNKS, 2)), dma((CHUNKS, 2)),
            dma((NE,)), dma((NE,)),
            dma((NE,)), dma((NE,)),
            dma((NE,)), dma((NE,)),
            dma((NZ,)), dma((NZ,)),
            dma((NZ, 2)), dma((NZ, 2)),
            dma((NZ,)), dma((NZ,)),
        ],
        name="step_and_migrate",
        compiler_params=pltpu.CompilerParams(
            collective_id=0, has_side_effects=True, vmem_limit_bytes=58 << 20
        ),
    )(
        new_position,
        replica_item,
        replica_grads[0],
        partial_grads.reshape(ITEMS, R, 8 * C),
        weight.reshape(ITEMS, *slab),
        first_moment.reshape(ITEMS, *slab),
        second_moment.reshape(ITEMS, *slab),
    )
    return tuple(out.reshape(weight.shape) for out in outs)


def solution(mesh):
    in_specs = (
        P("dp", "expert", None, None, None),
        P("dp", "expert", None, None),
        P("expert"),
        P("expert", None, None, "dp"),
        P("expert", None, None, "dp"),
        P("expert", None, None, "dp"),
        P("expert", None),
    )
    out_specs = (
        P("expert", None, None, "dp"),
        P("expert", None, None, "dp"),
        P("expert", None, None, "dp"),
    )
    return jax.shard_map(
        per_device, mesh=mesh, in_specs=in_specs, out_specs=out_specs, check_vma=False
    )
```

```python
import functools

import jax
import jax.numpy as jnp
from jax import lax
from jax.experimental import pallas as pl
from jax.experimental.pallas import tpu as pltpu
from jax.sharding import PartitionSpec as P

STEP = 10

beta_one = 0.9
beta_two = 0.95
learn_rate = 0.003
decay_rate = 0.1
epsilon = 1e-08

MESH = pl.DeviceIdType.MESH
NZ, NY, NX = 8, 4, 4
NE = NZ * NY
ITEMS = 16
SLABS = ITEMS + 2
CHUNKS = (
    (0, 2, 0, 16), (2, 4, 0, 8), (6, 4, 0, 8), (10, 4, 0, 8), (14, 4, 0, 8), (2, 8, 8, 8), (10, 8, 8, 8),
)
R, C = 16, 896
H = R // 2

FAR = (0, 1, 7, 2, 6, 3, 5, 4)
ARRIVAL = (0, 1, 3, 2)
GROUPS = ((0, 1), (1, 2), (3, 2), (5, 3))
STRAIGHT = list(range(1, NZ))
ACROSS = [dy * NZ + a for a in (1, 2, 3, 4, 5, 6, 7, 0) for dy in (1, 3)]
OPPOSITE = [2 * NZ + a for a in (1, 2, 3, 4, 5, 6, 7, 0)]
ORDER = [dy * NZ + a for a in (1, 2, 3, 4, 5, 6, 7, 0) for dy in (0, 1, 3, 2) if (a, dy) != (0, 0)]


def kernel(
    pos_s, rit_s, rg_h, pg_h, w_h, m_h, v_h,
    rw, rmv, tab_o,
    gr, w_v, m_v, v_v, cs, cr, ra, rb, sm, ag, ch, sw, smv,
    info, infos, tab, inv_s, tab_s,
    ld, tabsem, core_ss, core_rs, a_ss, a_rs, b_ss, b_rs,
    iz_ss, iz_rs, iy_ss, iy_rs, w_ss, w_rs, mv_ss, mv_rs, gz_ss, gz_rs, gy_ss, gy_rs, gf_ss, gf_rs,
):
    e = lax.axis_index("expert")
    d = lax.axis_index("dp")
    z, y = e // NY, e % NY
    x, c = d // 2, d % 2
    x_next, x_prev, x_far = (x + 1) % NX, (x + 3) % NX, (x + 2) % NX

    def holder(q):
        return ((z + FAR[q % NZ]) % NZ) * NY + (y + q // NZ) % NY

    def at_expert(index):
        return (index, d)

    def at_x(index):
        return (e, index * 2 + c)

    other_core = (e, x * 2 + 1 - c)

    loads = [
        pltpu.make_async_copy(rg_h, gr.at[pl.ds(0, 2)], ld.at[0]),
        pltpu.make_async_copy(w_h, w_v, ld.at[9]),
        *[
            pltpu.make_async_copy(pg_h.at[pl.ds(2 * i - 2, 2)], gr.at[pl.ds(2 * i, 2)], ld.at[i])
            for i in range(1, 9)
        ],
        pltpu.make_async_copy(m_h, m_v, ld.at[10]),
        pltpu.make_async_copy(v_h, v_v, ld.at[11]),
    ]
    for load in loads:
        load.start()
    gr_loads = [loads[0]] + loads[2:10]

    sub = lax.broadcasted_iota(jnp.int32, (8, 128), 0)
    lane = lax.broadcasted_iota(jnp.int32, (8, 128), 1)
    tile = jnp.where(sub == 0, -1, 0)
    for j in range(ITEMS):
        place = pos_s[j % 2, j // 2]
        hit = lane == place // ITEMS
        tile = jnp.where(hit & (sub == 0), place % ITEMS, tile)
        tile = jnp.where(hit & (sub == 2), j, tile)
    for k in range(2):
        tile = jnp.where((sub == 1) & (lane == k), rit_s[k], tile)
    info[...] = tile
    infos[0, 0] = tile
    inv_copy = pltpu.make_async_copy(info, inv_s, tabsem.at[0])
    inv_copy.start()

    barrier = pltpu.get_barrier_semaphore()
    for q in ORDER:
        pl.semaphore_signal(barrier, inc=1, device_id=at_expert(holder(q)), device_id_type=MESH)
    for peer in (other_core, at_x(x_next), at_x(x_prev)):
        pl.semaphore_signal(barrier, inc=1, device_id=peer, device_id_type=MESH)

    sends = []

    def send(src, dst, ss, rs, peer):
        copy = pltpu.make_async_remote_copy(
            src_ref=src, dst_ref=dst, send_sem=ss, recv_sem=rs, device_id=peer, device_id_type=MESH
        )
        copy.start()
        sends.append(copy)
        return copy

    core_copy, a_copy, b_copy = {}, {}, {}

    loaded = set()

    def widen(i):
        first, count, top, rows = CHUNKS[i]
        for u in range(first, first + count):
            if u // 2 not in loaded:
                loaded.add(u // 2)
                gr_loads[u // 2].wait()
            for xd in range(NX):
                columns = pl.ds(pl.multiple_of((xd * 2 + 1 - c) * C, 128), C)
                cs[u, xd, top : top + rows] = gr[u, :, columns].astype(jnp.float32)[top : top + rows]

    def stage_core(i):
        first, count, top, rows = CHUNKS[i]
        part = (pl.ds(first, count), slice(None), pl.ds(top, rows))
        core_copy[i] = send(cs.at[part], cr.at[part], core_ss.at[i], core_rs.at[i], other_core)

    def stage_a(i):
        first, count, top, rows = CHUNKS[i]
        core_copy[i].wait_recv()
        for u in range(first, first + count):
            for xd in range(NX):
                columns = pl.ds(pl.multiple_of((xd * 2 + c) * C, 128), C)
                own = gr[u, :, columns].astype(jnp.float32)[top : top + rows]
                cr[u, xd, top : top + rows] = cr[u, xd, top : top + rows] + own
        half = count // 2
        a_copy[i] = []
        for side, to in ((0, x_next), (1, x_prev)):
            units, part = pl.ds(first + side * half, half), pl.ds(top, rows)
            a_copy[i].append(
                send(cr.at[units, x_far, part], ra.at[units, part], a_ss.at[i, side], a_rs.at[i, side], at_x(to))
            )

    def stage_b(i):
        first, count, top, rows = CHUNKS[i]
        half = count // 2
        b_copy[i] = []
        for side, to in ((0, x_next), (1, x_prev)):
            a_copy[i][side].wait_recv()
            for u in range(first + side * half, first + side * half + half):
                cr[u, to, top : top + rows] = cr[u, to, top : top + rows] + ra[u, top : top + rows]
            units, part = pl.ds(first, count), pl.ds(top, rows)
            b_copy[i].append(
                send(cr.at[units, to, part], rb.at[side, units, part], b_ss.at[i, side], b_rs.at[i, side], at_x(to))
            )

    def stage_sum(i):
        first, count, top, rows = CHUNKS[i]
        b_copy[i][0].wait_recv()
        b_copy[i][1].wait_recv()
        for u in range(first, first + count):
            part = slice(top, top + rows)
            total = cr[u, x, part] + rb[0, u, part] + rb[1, u, part]
            if i == 0:
                for h in range(2):
                    ag[h, 0, 0, u] = total[h * H : h * H + H]
            else:
                sm[u - 2, part] = total

    w_copy = {}

    def send_w(slots):
        for q in slots:
            to = holder(q)
            sw[q] = w_v[inv_s[2, to]]
            w_copy[q] = send(sw.at[q], rw.at[q], w_ss.at[q], w_rs.at[q], at_expert(to))

    iz_copy, iy_copy = {}, {}

    def info_z():
        for a in range(1, NZ):
            iz_copy[a] = send(info, infos.at[0, a], iz_ss.at[a], iz_rs.at[a], at_expert(holder(a)))

    def info_y():
        for a in range(1, NZ):
            iz_copy[a].wait_recv()
        for dy in range(1, NY):
            iy_copy[dy] = send(
                infos.at[0], infos.at[dy], iy_ss.at[dy], iy_rs.at[dy], at_expert(holder(dy * NZ))
            )

    gz_copy, gy_copy, gf_copy = {}, {}, {}

    def gather_z(h):
        for a in range(1, NZ):
            gz_copy[h, a] = send(
                ag.at[h, 0, 0], ag.at[h, 0, a], gz_ss.at[h, a], gz_rs.at[h, a], at_expert(holder(a))
            )

    def gather_y(h, g):
        first, count = GROUPS[g]
        part = pl.ds(first, count)
        for a in range(max(first, 1), first + count):
            gz_copy[h, a].wait_recv()
        gy_copy[h, g] = [
            send(
                ag.at[h, 0, part], ag.at[h, dy, part], gy_ss.at[h, g, dy], gy_rs.at[h, g, dy],
                at_expert(holder(dy * NZ)),
            )
            for dy in (1, 3)
        ]

    def forward_y(h, g):
        first, count = GROUPS[g]
        part = pl.ds(first, count)
        gy_copy[h, g][0].wait_recv()
        gy_copy[h, g][1].wait_recv()
        dy = 1 if g in (0, 3) else 3
        gf_copy[h, g] = send(
            ag.at[h, dy, part], ag.at[h, 2, part], gf_ss.at[h, g], gf_rs.at[h, g], at_expert(holder(dy * NZ))
        )

    tab_copy = pltpu.make_async_copy(tab, tab_s, tabsem.at[1])

    def tables():
        for dy in range(1, NY):
            iy_copy[dy].wait_recv()
        sub = lax.broadcasted_iota(jnp.int32, (NE, 128), 0)
        lane = lax.broadcasted_iota(jnp.int32, (NE, 128), 1)
        place_rows = jnp.concatenate([infos[dy, :, 0, :] for dy in range(NY)], axis=0)
        places = jnp.sum(jnp.where(lane == e, place_rows, 0), axis=1, keepdims=True)
        tab[0:1, :] = jnp.max(jnp.where(places == lane, sub, 0), axis=0, keepdims=True)
        served = []
        for dy in ARRIVAL:
            rows = infos[dy, :, 1, :]
            for k in range(2):
                served.append(jnp.sum(jnp.where(lane[:NZ] == k, rows, 0), axis=1, keepdims=True))
        column = jnp.concatenate(served, axis=0)
        sub = lax.broadcasted_iota(jnp.int32, (2 * NE, 128), 0)
        lane = lax.broadcasted_iota(jnp.int32, (2 * NE, 128), 1)
        row = jnp.sum(jnp.where(sub == lane, column, 0), axis=0, keepdims=True)
        tab[1:2, :] = jnp.max(jnp.where((column == row) & (sub < lane), sub + 1, 0), axis=0, keepdims=True)
        tab[2:3, :] = jnp.max(jnp.where(column == lane + e * ITEMS, sub + 1, 0), axis=0, keepdims=True)
        tab[3:8, :] = jnp.zeros((5, 128), jnp.int32)
        tab_copy.start()

    def chain(h, order):
        dy = ARRIVAL[order]
        for k in range(2):
            for a in range(NZ):
                r = (order * 2 + k) * NZ + a
                ch[h, r + 1] = ag[h, dy, a, k] + ch[h, tab_s[1, r]]

    mv_copy = {}

    def moments(h, q, to):
        j = inv_s[2, to]
        part = slice(h * H, h * H + H)
        gradient = sm[j, part] + ch[h, tab_s[2, j]]
        smv[h, q, 0] = beta_one * m_v[j, part] + (1.0 - beta_one) * gradient
        smv[h, q, 1] = beta_two * v_v[j, part] + (1.0 - beta_two) * gradient * gradient

    def send_moments(h):
        for q in ORDER:
            to = holder(q)
            moments(h, q, to)
            mv_copy[h, q] = send(
                smv.at[h, q], rmv.at[h, q], mv_ss.at[h, q], mv_rs.at[h, q], at_expert(to)
            )
        moments(h, 0, e)

    widen(0)
    widen(1)
    loads[1].wait()
    inv_copy.wait()
    pl.semaphore_wait(barrier, NE - 1 + 3)
    stage_core(0)
    stage_core(1)
    send_w(STRAIGHT)
    info_z()
    stage_a(0)
    widen(2)
    stage_core(2)
    stage_b(0)
    stage_a(1)
    widen(3)
    stage_core(3)
    stage_sum(0)
    gather_z(0)
    gather_y(0, 0)
    gather_z(1)
    stage_b(1)
    stage_a(2)
    widen(4)
    stage_core(4)
    send_w(ACROSS[:4])
    gather_y(0, 1)
    info_y()
    stage_b(2)
    stage_a(3)
    widen(5)
    stage_core(5)
    stage_sum(1)
    gather_y(0, 2)
    forward_y(0, 0)
    stage_b(3)
    stage_a(4)
    send_w(ACROSS[4:8])
    gather_y(0, 3)
    forward_y(0, 1)
    stage_sum(2)
    widen(6)
    stage_core(6)
    tables()
    send_w(ACROSS[8:])
    stage_b(4)
    stage_a(5)
    forward_y(0, 2)
    stage_sum(3)
    for h in range(2):
        ch[h, 0] = jnp.zeros((H, C), jnp.float32)
    loads[10].wait()
    loads[11].wait()
    forward_y(0, 3)
    gather_y(1, 0)
    gather_y(1, 1)
    stage_b(5)
    stage_a(6)
    gather_y(1, 2)
    gather_y(1, 3)
    stage_sum(4)
    tab_copy.wait()
    for order in range(3):
        chain(0, order)
    for g in range(len(GROUPS)):
        gf_copy[0, g].wait_recv()
    chain(0, 3)
    send_moments(0)
    for g in range(len(GROUPS)):
        forward_y(1, g)
    stage_b(6)
    send_w(OPPOSITE)
    stage_sum(5)
    stage_sum(6)
    for order in range(3):
        chain(1, order)
    for g in range(len(GROUPS)):
        gf_copy[1, g].wait_recv()
    chain(1, 3)
    send_moments(1)

    sw[0] = w_v[inv_s[2, e]]
    own = [
        pltpu.make_async_copy(smv.at[0, 0], rmv.at[0, 0], ld.at[0]),
        pltpu.make_async_copy(smv.at[1, 0], rmv.at[1, 0], ld.at[2]),
        pltpu.make_async_copy(sw.at[0], rw.at[0], ld.at[1]),
    ]
    for copy in own:
        copy.start()
    tab_o[...] = tab[...]

    for q in ORDER:
        w_copy[q].wait_recv()
    for h in range(2):
        for q in ORDER:
            mv_copy[h, q].wait_recv()
    for copy in own:
        copy.wait()
    for copy in sends:
        copy.wait_send()


def place(tab_s, rw, rmv, ow, om, ov, w_v, mv_v, o_v, w_in, mv_in, w_out, m_out, v_out):
    ins, outs = [], []
    for p in range(ITEMS):
        q = tab_s[0, p]
        ins.append([
            pltpu.make_async_copy(rmv.at[0, q], mv_v.at[:, p, pl.ds(0, H)], mv_in.at[p, 0]),
            pltpu.make_async_copy(rmv.at[1, q], mv_v.at[:, p, pl.ds(H, H)], mv_in.at[p, 1]),
            pltpu.make_async_copy(rw.at[q], w_v.at[p], w_in.at[p]),
        ])
        for copy in ins[p]:
            copy.start()
    for p in range(ITEMS):
        for copy in ins[p]:
            copy.wait()
        first, second, weight = mv_v[0, p], mv_v[1, p], w_v[p]
        first_hat = first / (1.0 - beta_one**STEP)
        second_hat = second / (1.0 - beta_two**STEP)
        o_v[p] = weight - learn_rate * (
            first_hat / (jnp.sqrt(second_hat) + epsilon) + decay_rate * weight
        )
        for src, dst, sem in (
            (mv_v.at[0, p], om.at[p], m_out.at[p]),
            (mv_v.at[1, p], ov.at[p], v_out.at[p]),
            (o_v.at[p], ow.at[p], w_out.at[p]),
        ):
            outs.append(pltpu.make_async_copy(src, dst, sem))
            outs[-1].start()
    for copy in outs:
        copy.wait()


def per_device(
    partial_grads, replica_grads, replica_item, weight, first_moment, second_moment, new_position
):
    f32, i32, bf16 = jnp.float32, jnp.int32, jnp.bfloat16
    vmem, smem, dma = pltpu.VMEM, pltpu.SMEM, pltpu.SemaphoreType.DMA
    slab, half = (R, C), (H, C)
    anywhere = pl.BlockSpec(memory_space=pl.ANY)
    in_smem = pl.BlockSpec(memory_space=pltpu.SMEM)
    in_vmem = pl.BlockSpec(memory_space=pltpu.VMEM)
    rw, rmv, tab = pl.pallas_call(
        kernel,
        out_shape=[
            jax.ShapeDtypeStruct((NE, *slab), f32),
            jax.ShapeDtypeStruct((2, NE, 2, *half), f32),
            jax.ShapeDtypeStruct((8, 128), i32),
        ],
        in_specs=[in_smem, in_smem] + [anywhere] * 5,
        out_specs=[anywhere, anywhere, in_vmem],
        scratch_shapes=[
            vmem((SLABS, R, 8 * C), bf16),
            vmem((ITEMS, *slab), f32),
            vmem((ITEMS, *slab), f32),
            vmem((ITEMS, *slab), f32),
            vmem((SLABS, NX, *slab), f32),
            vmem((SLABS, NX, *slab), f32),
            vmem((SLABS, *slab), f32),
            vmem((2, SLABS, *slab), f32),
            vmem((ITEMS, *slab), f32),
            vmem((2, NY, NZ, 2, *half), f32),
            vmem((2, 2 * NE + 1, *half), f32),
            vmem((NE, *slab), f32),
            vmem((2, NE, 2, *half), f32),
            vmem((8, 128), i32),
            vmem((NY, NZ, 8, 128), i32),
            vmem((8, 128), i32),
            smem((8, 128), i32),
            smem((8, 128), i32),
            dma((12,)),
            dma((2,)),
            dma((len(CHUNKS),)), dma((len(CHUNKS),)),
            dma((len(CHUNKS), 2)), dma((len(CHUNKS), 2)),
            dma((len(CHUNKS), 2)), dma((len(CHUNKS), 2)),
            dma((NZ,)), dma((NZ,)),
            dma((NY,)), dma((NY,)),
            dma((NE,)), dma((NE,)),
            dma((2, NE)), dma((2, NE)),
            dma((2, NZ)), dma((2, NZ)),
            dma((2, len(GROUPS), NY)), dma((2, len(GROUPS), NY)),
            dma((2, len(GROUPS))), dma((2, len(GROUPS))),
        ],
        name="step_and_migrate",
        compiler_params=pltpu.CompilerParams(
            collective_id=0, has_side_effects=True, vmem_limit_bytes=58 << 20
        ),
    )(
        new_position.T,
        replica_item,
        replica_grads[0],
        partial_grads.reshape(ITEMS, R, 8 * C),
        weight.reshape(ITEMS, *slab),
        first_moment.reshape(ITEMS, *slab),
        second_moment.reshape(ITEMS, *slab),
    )
    outs = pl.pallas_call(
        place,
        out_shape=[jax.ShapeDtypeStruct((ITEMS, *slab), f32)] * 3,
        in_specs=[in_smem, anywhere, anywhere],
        out_specs=[anywhere] * 3,
        scratch_shapes=[
            vmem((ITEMS, *slab), f32),
            vmem((2, ITEMS, *slab), f32),
            vmem((ITEMS, *slab), f32),
            dma((ITEMS,)),
            dma((ITEMS, 2)),
        ]
        + [dma((ITEMS,))] * 3,
        name="place",
        compiler_params=pltpu.CompilerParams(vmem_limit_bytes=58 << 20),
    )(tab, rw, rmv)
    return tuple(out.reshape(weight.shape) for out in outs)


def solution(mesh):
    in_specs = (
        P("dp", "expert", None, None, None),
        P("dp", "expert", None, None),
        P("expert"),
        P("expert", None, None, "dp"),
        P("expert", None, None, "dp"),
        P("expert", None, None, "dp"),
        P("expert", None),
    )
    out_specs = (
        P("expert", None, None, "dp"),
        P("expert", None, None, "dp"),
        P("expert", None, None, "dp"),
    )
    return jax.shard_map(
        per_device, mesh=mesh, in_specs=in_specs, out_specs=out_specs, check_vma=False
    )
```

```python
import functools

import jax
import jax.numpy as jnp
from jax import lax
from jax.experimental import pallas as pl
from jax.experimental.pallas import tpu as pltpu
from jax.sharding import PartitionSpec as P

STEP = 10

beta_one = 0.9
beta_two = 0.95
learn_rate = 0.003
decay_rate = 0.1
epsilon = 1e-08

MESH = pl.DeviceIdType.MESH
NZ, NY, NX = 8, 4, 4
NE = NZ * NY
ITEMS = 16
SLABS = ITEMS + 2
CHUNKS = (
    (0, 2, 0, 16), (2, 4, 0, 8), (6, 4, 0, 8), (10, 4, 0, 8), (14, 4, 0, 8), (2, 8, 8, 8), (10, 8, 8, 8),
)
R, C = 16, 896
H = R // 2

FAR = (0, 1, 7, 2, 6, 3, 5, 4)
ARRIVAL = (0, 1, 3, 2)
GROUPS = ((0, 1), (1, 2), (3, 2), (5, 3))
ORDER = [dy * NZ + a for a in (7, 6, 5, 4, 3, 2, 1, 0) for dy in (2, 1, 3, 0) if (a, dy) != (0, 0)]


def kernel(
    pos_s, rit_s, rg_h, pg_h, w_h, m_h, v_h,
    rw, rmv, tab_o,
    gr, w_v, m_v, v_v, cs, cr, ra, rb, sm, ag, ch, sw, smv,
    info, infos, tab, inv_s, tab_s,
    ld, tabsem, core_ss, core_rs, a_ss, a_rs, b_ss, b_rs,
    iz_ss, iz_rs, iy_ss, iy_rs, w_ss, w_rs, mv_ss, mv_rs, gz_ss, gz_rs, gy_ss, gy_rs,
):
    e = lax.axis_index("expert")
    d = lax.axis_index("dp")
    z, y = e // NY, e % NY
    x, c = d // 2, d % 2
    x_next, x_prev, x_far = (x + 1) % NX, (x + 3) % NX, (x + 2) % NX

    def holder(q):
        return ((z + FAR[q % NZ]) % NZ) * NY + (y + q // NZ) % NY

    def slot_at(a, dy):
        odd = a % 2
        dz = odd * ((a + 1) // 2) + (1 - odd) * (NZ - a // 2)
        return dy * NZ + a, ((z + dz) % NZ) * NY + (y + dy) % NY

    def at_expert(index):
        return (index, d)

    def at_x(index):
        return (e, index * 2 + c)

    other_core = (e, x * 2 + 1 - c)

    loads = [
        pltpu.make_async_copy(rg_h, gr.at[pl.ds(0, 2)], ld.at[0]),
        pltpu.make_async_copy(w_h, w_v, ld.at[9]),
        *[
            pltpu.make_async_copy(pg_h.at[pl.ds(2 * i - 2, 2)], gr.at[pl.ds(2 * i, 2)], ld.at[i])
            for i in range(1, 9)
        ],
        pltpu.make_async_copy(m_h, m_v, ld.at[10]),
        pltpu.make_async_copy(v_h, v_v, ld.at[11]),
    ]
    for load in loads:
        load.start()
    gr_loads = [loads[0]] + loads[2:10]

    sub = lax.broadcasted_iota(jnp.int32, (8, 128), 0)
    lane = lax.broadcasted_iota(jnp.int32, (8, 128), 1)
    tile = jnp.where(sub == 0, -1, 0)
    for j in range(ITEMS):
        place = pos_s[j % 2, j // 2]
        hit = lane == place // ITEMS
        tile = jnp.where(hit & (sub == 0), place % ITEMS, tile)
        tile = jnp.where(hit & (sub == 2), j, tile)
    for k in range(2):
        tile = jnp.where((sub == 1) & (lane == k), rit_s[k], tile)
    info[...] = tile
    infos[0, 0] = tile
    inv_copy = pltpu.make_async_copy(info, inv_s, tabsem.at[0])
    inv_copy.start()

    barrier = pltpu.get_barrier_semaphore()

    @pl.loop(0, NE - 1)
    def _(i):
        _, to = slot_at(NZ - 1 - i // NY, NY - 1 - i % NY)
        pl.semaphore_signal(barrier, inc=1, device_id=at_expert(to), device_id_type=MESH)

    for peer in (other_core, at_x(x_next), at_x(x_prev)):
        pl.semaphore_signal(barrier, inc=1, device_id=peer, device_id_type=MESH)

    sends = []

    def send(src, dst, ss, rs, peer):
        copy = pltpu.make_async_remote_copy(
            src_ref=src, dst_ref=dst, send_sem=ss, recv_sem=rs, device_id=peer, device_id_type=MESH
        )
        copy.start()
        sends.append(copy)
        return copy

    core_copy, a_copy, b_copy = {}, {}, {}

    loaded = set()

    def widen(i):
        first, count, top, rows = CHUNKS[i]
        for pair in range(first // 2, (first + count) // 2):
            if pair not in loaded:
                loaded.add(pair)
                gr_loads[pair].wait()

        @pl.loop(first, first + count)
        def _(u):
            @pl.loop(0, NX)
            def _(xd):
                columns = pl.ds(pl.multiple_of((xd * 2 + 1 - c) * C, 128), C)
                cs[u, xd, top : top + rows] = gr[u, :, columns].astype(jnp.float32)[top : top + rows]

    def stage_core(i):
        first, count, top, rows = CHUNKS[i]
        part = (pl.ds(first, count), slice(None), pl.ds(top, rows))
        core_copy[i] = send(cs.at[part], cr.at[part], core_ss.at[i], core_rs.at[i], other_core)

    def stage_a(i):
        first, count, top, rows = CHUNKS[i]
        core_copy[i].wait_recv()

        @pl.loop(first, first + count)
        def _(u):
            @pl.loop(0, NX)
            def _(xd):
                columns = pl.ds(pl.multiple_of((xd * 2 + c) * C, 128), C)
                own = gr[u, :, columns].astype(jnp.float32)[top : top + rows]
                cr[u, xd, top : top + rows] = cr[u, xd, top : top + rows] + own

        half = count // 2
        a_copy[i] = []
        for side, to in ((0, x_next), (1, x_prev)):
            units, part = pl.ds(first + side * half, half), pl.ds(top, rows)
            a_copy[i].append(
                send(cr.at[units, x_far, part], ra.at[units, part], a_ss.at[i, side], a_rs.at[i, side], at_x(to))
            )

    def stage_b(i):
        first, count, top, rows = CHUNKS[i]
        half = count // 2
        b_copy[i] = []
        for side, to in ((0, x_next), (1, x_prev)):
            a_copy[i][side].wait_recv()

            @pl.loop(first + side * half, first + side * half + half)
            def _(u):
                cr[u, to, top : top + rows] = cr[u, to, top : top + rows] + ra[u, top : top + rows]

            units, part = pl.ds(first, count), pl.ds(top, rows)
            b_copy[i].append(
                send(cr.at[units, to, part], rb.at[side, units, part], b_ss.at[i, side], b_rs.at[i, side], at_x(to))
            )

    def stage_sum(i):
        first, count, top, rows = CHUNKS[i]
        b_copy[i][0].wait_recv()
        b_copy[i][1].wait_recv()

        @pl.loop(first, first + count)
        def _(u):
            part = slice(top, top + rows)
            total = cr[u, x, part] + rb[0, u, part] + rb[1, u, part]
            if i == 0:
                for h in range(2):
                    ag[h, 0, 0, u] = total[h * H : h * H + H]
            else:
                sm[u - 2, part] = total


    def w_send(q, to):
        return pltpu.make_async_remote_copy(
            src_ref=sw.at[q], dst_ref=rw.at[q], send_sem=w_ss.at[q], recv_sem=w_rs.at[q],
            device_id=at_expert(to), device_id_type=MESH,
        )

    def send_w(dys, start, stop):
        @pl.loop(start, stop)
        def _(i):
            a, dy = (1 + i // len(dys)) % NZ, dys[0] + 2 * (i % len(dys))
            q, to = slot_at(a, dy)
            sw[q] = w_v[inv_s[2, to]]
            w_send(q, to).start()

    iz_copy, iy_copy = {}, {}

    def info_z():
        for a in range(1, NZ):
            iz_copy[a] = send(info, infos.at[0, a], iz_ss.at[a], iz_rs.at[a], at_expert(holder(a)))

    def info_y():
        for a in range(1, NZ):
            iz_copy[a].wait_recv()
        for dy in range(1, NY):
            iy_copy[dy] = send(
                infos.at[0], infos.at[dy], iy_ss.at[dy], iy_rs.at[dy], at_expert(holder(dy * NZ))
            )

    gz_copy, gy_copy = {}, {}

    def gather_z(h):
        for a in range(1, NZ):
            gz_copy[h, a] = send(
                ag.at[h, 0, 0], ag.at[h, 0, a], gz_ss.at[h, a], gz_rs.at[h, a], at_expert(holder(a))
            )

    def gather_y(h, g):
        first, count = GROUPS[g]
        part = pl.ds(first, count)
        for a in range(max(first, 1), first + count):
            gz_copy[h, a].wait_recv()
        gy_copy[h, g] = [
            send(
                ag.at[h, 0, part], ag.at[h, dy, part], gy_ss.at[h, g, dy], gy_rs.at[h, g, dy],
                at_expert(holder(dy * NZ)),
            )
            for dy in (2, 1, 3)
        ]

    tab_copy = pltpu.make_async_copy(tab, tab_s, tabsem.at[1])

    def tables():
        for dy in range(1, NY):
            iy_copy[dy].wait_recv()
        sub = lax.broadcasted_iota(jnp.int32, (NE, 128), 0)
        lane = lax.broadcasted_iota(jnp.int32, (NE, 128), 1)
        place_rows = jnp.concatenate([infos[dy, :, 0, :] for dy in range(NY)], axis=0)
        places = jnp.sum(jnp.where(lane == e, place_rows, 0), axis=1, keepdims=True)
        tab[0:1, :] = jnp.max(jnp.where(places == lane, sub, 0), axis=0, keepdims=True)
        served = []
        for dy in ARRIVAL:
            rows = infos[dy, :, 1, :]
            for k in range(2):
                served.append(jnp.sum(jnp.where(lane[:NZ] == k, rows, 0), axis=1, keepdims=True))
        column = jnp.concatenate(served, axis=0)
        sub = lax.broadcasted_iota(jnp.int32, (2 * NE, 128), 0)
        lane = lax.broadcasted_iota(jnp.int32, (2 * NE, 128), 1)
        row = jnp.sum(jnp.where(sub == lane, column, 0), axis=0, keepdims=True)
        tab[1:2, :] = jnp.max(jnp.where((column == row) & (sub < lane), sub + 1, 0), axis=0, keepdims=True)
        tab[2:3, :] = jnp.max(jnp.where(column == lane + e * ITEMS, sub + 1, 0), axis=0, keepdims=True)
        tab[3:8, :] = jnp.zeros((5, 128), jnp.int32)
        tab_copy.start()

    def chain(h, order):
        dy = ARRIVAL[order]

        @pl.loop(0, 2 * NZ)
        def _(i):
            r = order * 2 * NZ + i
            ch[h, r + 1] = ag[h, dy, i % NZ, i // NZ] + ch[h, tab_s[1, r]]

    mv_copy = {}

    def moments(h, q, to):
        j = inv_s[2, to]
        part = slice(h * H, h * H + H)
        gradient = sm[j, part] + ch[h, tab_s[2, j]]
        smv[h, q, 0] = beta_one * m_v[j, part] + (1.0 - beta_one) * gradient
        smv[h, q, 1] = beta_two * v_v[j, part] + (1.0 - beta_two) * gradient * gradient

    def moments_copy(h, q, to):
        return pltpu.make_async_remote_copy(
            src_ref=smv.at[h, q], dst_ref=rmv.at[h, q], send_sem=mv_ss.at[h, q], recv_sem=mv_rs.at[h, q],
            device_id=at_expert(to), device_id_type=MESH,
        )

    def send_moments(h):
        @pl.loop(0, NE - 1)
        def _(i):
            q, to = slot_at(NZ - 1 - i // NY, NY - 1 - i % NY)
            moments(h, q, to)
            moments_copy(h, q, to).start()

        for q in ORDER:
            mv_copy[h, q] = moments_copy(h, q, holder(q))
            sends.append(mv_copy[h, q])
        moments(h, 0, e)

    widen(0)
    widen(1)
    loads[1].wait()
    inv_copy.wait()
    pl.semaphore_wait(barrier, NE - 1 + 3)
    stage_core(0)
    stage_core(1)
    send_w((0,), 0, NZ - 1)
    send_w((1, 3), 0, 2 * NZ)
    send_w((2,), 0, NZ)
    info_z()
    stage_a(0)
    widen(2)
    stage_core(2)
    stage_b(0)
    stage_a(1)
    widen(3)
    stage_core(3)
    stage_sum(0)
    gather_z(0)
    gather_y(0, 0)
    gather_z(1)
    stage_b(1)
    stage_a(2)
    widen(4)
    stage_core(4)
    gather_y(0, 1)
    info_y()
    stage_b(2)
    stage_a(3)
    widen(5)
    stage_core(5)
    stage_sum(1)
    gather_y(0, 2)
    stage_b(3)
    stage_a(4)
    gather_y(0, 3)
    stage_sum(2)
    widen(6)
    stage_core(6)
    tables()
    stage_b(4)
    stage_a(5)
    stage_sum(3)
    for h in range(2):
        ch[h, 0] = jnp.zeros((H, C), jnp.float32)
    loads[10].wait()
    loads[11].wait()
    gather_y(1, 0)
    gather_y(1, 1)
    stage_b(5)
    stage_a(6)
    gather_y(1, 2)
    gather_y(1, 3)
    stage_sum(4)
    tab_copy.wait()
    chain(0, 0)
    for g in range(len(GROUPS)):
        for copy in gy_copy[0, g]:
            copy.wait_recv()
    for order in range(1, NY):
        chain(0, order)
    send_moments(0)
    stage_b(6)
    stage_sum(5)
    stage_sum(6)
    chain(1, 0)
    for g in range(len(GROUPS)):
        for copy in gy_copy[1, g]:
            copy.wait_recv()
    for order in range(1, NY):
        chain(1, order)
    send_moments(1)

    sw[0] = w_v[inv_s[2, e]]
    own = [
        pltpu.make_async_copy(smv.at[0, 0], rmv.at[0, 0], ld.at[0]),
        pltpu.make_async_copy(smv.at[1, 0], rmv.at[1, 0], ld.at[2]),
        pltpu.make_async_copy(sw.at[0], rw.at[0], ld.at[1]),
    ]
    for copy in own:
        copy.start()
    tab_o[...] = tab[...]

    for q in ORDER:
        w_copy = w_send(q, holder(q))
        w_copy.wait_recv()
        w_copy.wait_send()
    for h in range(2):
        for q in ORDER:
            mv_copy[h, q].wait_recv()
    for copy in own:
        copy.wait()
    for copy in sends:
        copy.wait_send()


def place(tab_s, rw, rmv, ow, om, ov, w_v, mv_v, o_v, w_in, mv_in, w_out, m_out, v_out):
    ins, outs = [], []
    for p in range(ITEMS):
        q = tab_s[0, p]
        ins.append([
            pltpu.make_async_copy(rmv.at[0, q], mv_v.at[:, p, pl.ds(0, H)], mv_in.at[p, 0]),
            pltpu.make_async_copy(rmv.at[1, q], mv_v.at[:, p, pl.ds(H, H)], mv_in.at[p, 1]),
            pltpu.make_async_copy(rw.at[q], w_v.at[p], w_in.at[p]),
        ])
        for copy in ins[p]:
            copy.start()
    for p in range(ITEMS):
        for copy in ins[p]:
            copy.wait()
        first, second, weight = mv_v[0, p], mv_v[1, p], w_v[p]
        first_hat = first / (1.0 - beta_one**STEP)
        second_hat = second / (1.0 - beta_two**STEP)
        o_v[p] = weight - learn_rate * (
            first_hat / (jnp.sqrt(second_hat) + epsilon) + decay_rate * weight
        )
        for src, dst, sem in (
            (mv_v.at[0, p], om.at[p], m_out.at[p]),
            (mv_v.at[1, p], ov.at[p], v_out.at[p]),
            (o_v.at[p], ow.at[p], w_out.at[p]),
        ):
            outs.append(pltpu.make_async_copy(src, dst, sem))
            outs[-1].start()
    for copy in outs:
        copy.wait()


def per_device(
    partial_grads, replica_grads, replica_item, weight, first_moment, second_moment, new_position
):
    f32, i32, bf16 = jnp.float32, jnp.int32, jnp.bfloat16
    vmem, smem, dma = pltpu.VMEM, pltpu.SMEM, pltpu.SemaphoreType.DMA
    slab, half = (R, C), (H, C)
    anywhere = pl.BlockSpec(memory_space=pl.ANY)
    in_smem = pl.BlockSpec(memory_space=pltpu.SMEM)
    in_vmem = pl.BlockSpec(memory_space=pltpu.VMEM)
    rw, rmv, tab = pl.pallas_call(
        kernel,
        out_shape=[
            jax.ShapeDtypeStruct((NE, *slab), f32),
            jax.ShapeDtypeStruct((2, NE, 2, *half), f32),
            jax.ShapeDtypeStruct((8, 128), i32),
        ],
        in_specs=[in_smem, in_smem] + [anywhere] * 5,
        out_specs=[anywhere, anywhere, in_vmem],
        scratch_shapes=[
            vmem((SLABS, R, 8 * C), bf16),
            vmem((ITEMS, *slab), f32),
            vmem((ITEMS, *slab), f32),
            vmem((ITEMS, *slab), f32),
            vmem((SLABS, NX, *slab), f32),
            vmem((SLABS, NX, *slab), f32),
            vmem((SLABS, *slab), f32),
            vmem((2, SLABS, *slab), f32),
            vmem((ITEMS, *slab), f32),
            vmem((2, NY, NZ, 2, *half), f32),
            vmem((2, 2 * NE + 1, *half), f32),
            vmem((NE, *slab), f32),
            vmem((2, NE, 2, *half), f32),
            vmem((8, 128), i32),
            vmem((NY, NZ, 8, 128), i32),
            vmem((8, 128), i32),
            smem((8, 128), i32),
            smem((8, 128), i32),
            dma((12,)),
            dma((2,)),
            dma((len(CHUNKS),)), dma((len(CHUNKS),)),
            dma((len(CHUNKS), 2)), dma((len(CHUNKS), 2)),
            dma((len(CHUNKS), 2)), dma((len(CHUNKS), 2)),
            dma((NZ,)), dma((NZ,)),
            dma((NY,)), dma((NY,)),
            dma((NE,)), dma((NE,)),
            dma((2, NE)), dma((2, NE)),
            dma((2, NZ)), dma((2, NZ)),
            dma((2, len(GROUPS), NY)), dma((2, len(GROUPS), NY)),
        ],
        name="step_and_migrate",
        compiler_params=pltpu.CompilerParams(
            collective_id=0, has_side_effects=True, vmem_limit_bytes=58 << 20
        ),
    )(
        new_position.T,
        replica_item,
        replica_grads[0],
        partial_grads.reshape(ITEMS, R, 8 * C),
        weight.reshape(ITEMS, *slab),
        first_moment.reshape(ITEMS, *slab),
        second_moment.reshape(ITEMS, *slab),
    )
    outs = pl.pallas_call(
        place,
        out_shape=[jax.ShapeDtypeStruct((ITEMS, *slab), f32)] * 3,
        in_specs=[in_smem, anywhere, anywhere],
        out_specs=[anywhere] * 3,
        scratch_shapes=[
            vmem((ITEMS, *slab), f32),
            vmem((2, ITEMS, *slab), f32),
            vmem((ITEMS, *slab), f32),
            dma((ITEMS,)),
            dma((ITEMS, 2)),
        ]
        + [dma((ITEMS,))] * 3,
        name="place",
        compiler_params=pltpu.CompilerParams(vmem_limit_bytes=58 << 20),
    )(tab, rw, rmv)
    return tuple(out.reshape(weight.shape) for out in outs)


def solution(mesh):
    in_specs = (
        P("dp", "expert", None, None, None),
        P("dp", "expert", None, None),
        P("expert"),
        P("expert", None, None, "dp"),
        P("expert", None, None, "dp"),
        P("expert", None, None, "dp"),
        P("expert", None),
    )
    out_specs = (
        P("expert", None, None, "dp"),
        P("expert", None, None, "dp"),
        P("expert", None, None, "dp"),
    )
    return jax.shard_map(
        per_device, mesh=mesh, in_specs=in_specs, out_specs=out_specs, check_vma=False
    )
```

```python
import functools

import jax
import jax.numpy as jnp
from jax import lax
from jax.experimental import pallas as pl
from jax.experimental.pallas import tpu as pltpu
from jax.sharding import PartitionSpec as P

STEP = 10

beta_one = 0.9
beta_two = 0.95
learn_rate = 0.003
decay_rate = 0.1
epsilon = 1e-08

MESH = pl.DeviceIdType.MESH
NZ, NY, NX = 8, 4, 4
NE = NZ * NY
ITEMS = 16
SLABS = ITEMS + 2
CHUNKS = (
    (0, 2, 0, 16), (2, 4, 0, 8), (6, 4, 0, 8), (10, 4, 0, 8), (14, 4, 0, 8), (2, 8, 8, 8), (10, 8, 8, 8),
)
R, C = 16, 896
H = R // 2

FAR = (0, 1, 7, 2, 6, 3, 5, 4)
ARRIVAL = (0, 1, 3, 2)
GROUPS = ((0, 1), (1, 2), (3, 2), (5, 3))
STRAIGHT = list(range(1, NZ))
ACROSS = [dy * NZ + a for a in (1, 2, 3, 4, 5, 6, 7, 0) for dy in (1, 3)]
OPPOSITE = [2 * NZ + a for a in (1, 2, 3, 4, 5, 6, 7, 0)]
ORDER = [dy * NZ + a for a in (7, 6, 5, 4, 3, 2, 1, 0) for dy in (2, 1, 3, 0) if (a, dy) != (0, 0)]


def kernel(
    pos_s, rit_s, rg_h, pg_h, w_h, m_h, v_h,
    rw, rmv, tab_o,
    gr, w_v, m_v, v_v, cs, cr, ra, rb, sm, ag, ch, sw, smv,
    info, infos, tab, inv_s, tab_s,
    ld, tabsem, core_ss, core_rs, a_ss, a_rs, b_ss, b_rs,
    iz_ss, iz_rs, iy_ss, iy_rs, w_ss, w_rs, mv_ss, mv_rs, gz_ss, gz_rs, gy_ss, gy_rs,
):
    e = lax.axis_index("expert")
    d = lax.axis_index("dp")
    z, y = e // NY, e % NY
    x, c = d // 2, d % 2
    x_next, x_prev, x_far = (x + 1) % NX, (x + 3) % NX, (x + 2) % NX

    def holder(q):
        return ((z + FAR[q % NZ]) % NZ) * NY + (y + q // NZ) % NY

    def at_expert(index):
        return (index, d)

    def at_x(index):
        return (e, index * 2 + c)

    other_core = (e, x * 2 + 1 - c)

    loads = [
        pltpu.make_async_copy(rg_h, gr.at[pl.ds(0, 2)], ld.at[0]),
        pltpu.make_async_copy(w_h, w_v, ld.at[9]),
        *[
            pltpu.make_async_copy(pg_h.at[pl.ds(2 * i - 2, 2)], gr.at[pl.ds(2 * i, 2)], ld.at[i])
            for i in range(1, 9)
        ],
        pltpu.make_async_copy(m_h, m_v, ld.at[10]),
        pltpu.make_async_copy(v_h, v_v, ld.at[11]),
    ]
    for load in loads:
        load.start()
    gr_loads = [loads[0]] + loads[2:10]

    sub = lax.broadcasted_iota(jnp.int32, (8, 128), 0)
    lane = lax.broadcasted_iota(jnp.int32, (8, 128), 1)
    tile = jnp.where(sub == 0, -1, 0)
    for j in range(ITEMS):
        place = pos_s[j % 2, j // 2]
        hit = lane == place // ITEMS
        tile = jnp.where(hit & (sub == 0), place % ITEMS, tile)
        tile = jnp.where(hit & (sub == 2), j, tile)
    for k in range(2):
        tile = jnp.where((sub == 1) & (lane == k), rit_s[k], tile)
    info[...] = tile
    infos[0, 0] = tile
    inv_copy = pltpu.make_async_copy(info, inv_s, tabsem.at[0])
    inv_copy.start()

    barrier = pltpu.get_barrier_semaphore()
    for q in ORDER:
        pl.semaphore_signal(barrier, inc=1, device_id=at_expert(holder(q)), device_id_type=MESH)
    for peer in (other_core, at_x(x_next), at_x(x_prev)):
        pl.semaphore_signal(barrier, inc=1, device_id=peer, device_id_type=MESH)

    sends = []

    def send(src, dst, ss, rs, peer):
        copy = pltpu.make_async_remote_copy(
            src_ref=src, dst_ref=dst, send_sem=ss, recv_sem=rs, device_id=peer, device_id_type=MESH
        )
        copy.start()
        sends.append(copy)
        return copy

    core_copy, a_copy, b_copy = {}, {}, {}

    loaded = set()

    def widen(i):
        first, count, top, rows = CHUNKS[i]
        for u in range(first, first + count):
            if u // 2 not in loaded:
                loaded.add(u // 2)
                gr_loads[u // 2].wait()
            for xd in range(NX):
                columns = pl.ds(pl.multiple_of((xd * 2 + 1 - c) * C, 128), C)
                cs[u, xd, top : top + rows] = gr[u, :, columns].astype(jnp.float32)[top : top + rows]

    def stage_core(i):
        first, count, top, rows = CHUNKS[i]
        part = (pl.ds(first, count), slice(None), pl.ds(top, rows))
        core_copy[i] = send(cs.at[part], cr.at[part], core_ss.at[i], core_rs.at[i], other_core)

    def stage_a(i):
        first, count, top, rows = CHUNKS[i]
        core_copy[i].wait_recv()
        for u in range(first, first + count):
            for xd in range(NX):
                columns = pl.ds(pl.multiple_of((xd * 2 + c) * C, 128), C)
                own = gr[u, :, columns].astype(jnp.float32)[top : top + rows]
                cr[u, xd, top : top + rows] = cr[u, xd, top : top + rows] + own
        half = count // 2
        a_copy[i] = []
        for side, to in ((0, x_next), (1, x_prev)):
            units, part = pl.ds(first + side * half, half), pl.ds(top, rows)
            a_copy[i].append(
                send(cr.at[units, x_far, part], ra.at[units, part], a_ss.at[i, side], a_rs.at[i, side], at_x(to))
            )

    def stage_b(i):
        first, count, top, rows = CHUNKS[i]
        half = count // 2
        b_copy[i] = []
        for side, to in ((0, x_next), (1, x_prev)):
            a_copy[i][side].wait_recv()
            for u in range(first + side * half, first + side * half + half):
                cr[u, to, top : top + rows] = cr[u, to, top : top + rows] + ra[u, top : top + rows]
            units, part = pl.ds(first, count), pl.ds(top, rows)
            b_copy[i].append(
                send(cr.at[units, to, part], rb.at[side, units, part], b_ss.at[i, side], b_rs.at[i, side], at_x(to))
            )

    def stage_sum(i):
        first, count, top, rows = CHUNKS[i]
        b_copy[i][0].wait_recv()
        b_copy[i][1].wait_recv()
        for u in range(first, first + count):
            part = slice(top, top + rows)
            total = cr[u, x, part] + rb[0, u, part] + rb[1, u, part]
            if i == 0:
                for h in range(2):
                    ag[h, 0, 0, u] = total[h * H : h * H + H]
            else:
                sm[u - 2, part] = total

    w_copy = {}

    def send_w(slots):
        for q in slots:
            to = holder(q)
            sw[q] = w_v[inv_s[2, to]]
            w_copy[q] = send(sw.at[q], rw.at[q], w_ss.at[q], w_rs.at[q], at_expert(to))

    iz_copy, iy_copy = {}, {}

    def info_z():
        for a in range(1, NZ):
            iz_copy[a] = send(info, infos.at[0, a], iz_ss.at[a], iz_rs.at[a], at_expert(holder(a)))

    def info_y():
        for a in range(1, NZ):
            iz_copy[a].wait_recv()
        for dy in range(1, NY):
            iy_copy[dy] = send(
                infos.at[0], infos.at[dy], iy_ss.at[dy], iy_rs.at[dy], at_expert(holder(dy * NZ))
            )

    gz_copy, gy_copy = {}, {}

    def gather_z(h):
        for a in range(1, NZ):
            gz_copy[h, a] = send(
                ag.at[h, 0, 0], ag.at[h, 0, a], gz_ss.at[h, a], gz_rs.at[h, a], at_expert(holder(a))
            )

    def gather_y(h, g):
        first, count = GROUPS[g]
        part = pl.ds(first, count)
        for a in range(max(first, 1), first + count):
            gz_copy[h, a].wait_recv()
        gy_copy[h, g] = [
            send(
                ag.at[h, 0, part], ag.at[h, dy, part], gy_ss.at[h, g, dy], gy_rs.at[h, g, dy],
                at_expert(holder(dy * NZ)),
            )
            for dy in (2, 1, 3)
        ]

    tab_copy = pltpu.make_async_copy(tab, tab_s, tabsem.at[1])

    def tables():
        for dy in range(1, NY):
            iy_copy[dy].wait_recv()
        sub = lax.broadcasted_iota(jnp.int32, (NE, 128), 0)
        lane = lax.broadcasted_iota(jnp.int32, (NE, 128), 1)
        place_rows = jnp.concatenate([infos[dy, :, 0, :] for dy in range(NY)], axis=0)
        places = jnp.sum(jnp.where(lane == e, place_rows, 0), axis=1, keepdims=True)
        tab[0:1, :] = jnp.max(jnp.where(places == lane, sub, 0), axis=0, keepdims=True)
        served = []
        for dy in ARRIVAL:
            rows = infos[dy, :, 1, :]
            for k in range(2):
                served.append(jnp.sum(jnp.where(lane[:NZ] == k, rows, 0), axis=1, keepdims=True))
        column = jnp.concatenate(served, axis=0)
        sub = lax.broadcasted_iota(jnp.int32, (2 * NE, 128), 0)
        lane = lax.broadcasted_iota(jnp.int32, (2 * NE, 128), 1)
        row = jnp.sum(jnp.where(sub == lane, column, 0), axis=0, keepdims=True)
        tab[1:2, :] = jnp.max(jnp.where((column == row) & (sub < lane), sub + 1, 0), axis=0, keepdims=True)
        tab[2:3, :] = jnp.max(jnp.where(column == lane + e * ITEMS, sub + 1, 0), axis=0, keepdims=True)
        tab[3:8, :] = jnp.zeros((5, 128), jnp.int32)
        tab_copy.start()

    def chain(h, order):
        dy = ARRIVAL[order]
        for k in range(2):
            for a in range(NZ):
                r = (order * 2 + k) * NZ + a
                ch[h, r + 1] = ag[h, dy, a, k] + ch[h, tab_s[1, r]]

    mv_copy = {}

    def moments(h, q, to):
        j = inv_s[2, to]
        part = slice(h * H, h * H + H)
        gradient = sm[j, part] + ch[h, tab_s[2, j]]
        smv[h, q, 0] = beta_one * m_v[j, part] + (1.0 - beta_one) * gradient
        smv[h, q, 1] = beta_two * v_v[j, part] + (1.0 - beta_two) * gradient * gradient

    def send_moments(h):
        for q in ORDER:
            to = holder(q)
            moments(h, q, to)
            mv_copy[h, q] = send(
                smv.at[h, q], rmv.at[h, q], mv_ss.at[h, q], mv_rs.at[h, q], at_expert(to)
            )
        moments(h, 0, e)

    widen(0)
    widen(1)
    loads[1].wait()
    inv_copy.wait()
    pl.semaphore_wait(barrier, NE - 1 + 3)
    stage_core(0)
    stage_core(1)
    send_w(STRAIGHT + ACROSS)
    info_z()
    stage_a(0)
    widen(2)
    stage_core(2)
    stage_b(0)
    stage_a(1)
    widen(3)
    stage_core(3)
    stage_sum(0)
    gather_z(0)
    gather_y(0, 0)
    gather_z(1)
    stage_b(1)
    stage_a(2)
    widen(4)
    stage_core(4)
    gather_y(0, 1)
    info_y()
    stage_b(2)
    stage_a(3)
    widen(5)
    stage_core(5)
    stage_sum(1)
    gather_y(0, 2)
    stage_b(3)
    stage_a(4)
    gather_y(0, 3)
    stage_sum(2)
    widen(6)
    stage_core(6)
    tables()
    stage_b(4)
    stage_a(5)
    send_w(OPPOSITE)
    stage_sum(3)
    for h in range(2):
        ch[h, 0] = jnp.zeros((H, C), jnp.float32)
    loads[10].wait()
    loads[11].wait()
    gather_y(1, 0)
    gather_y(1, 1)
    stage_b(5)
    stage_a(6)
    gather_y(1, 2)
    gather_y(1, 3)
    stage_sum(4)
    tab_copy.wait()
    chain(0, 0)
    for g in range(len(GROUPS)):
        for copy in gy_copy[0, g]:
            copy.wait_recv()
    for order in range(1, NY):
        chain(0, order)
    send_moments(0)
    stage_b(6)
    stage_sum(5)
    stage_sum(6)
    chain(1, 0)
    for g in range(len(GROUPS)):
        for copy in gy_copy[1, g]:
            copy.wait_recv()
    for order in range(1, NY):
        chain(1, order)
    send_moments(1)

    sw[0] = w_v[inv_s[2, e]]
    own = [
        pltpu.make_async_copy(smv.at[0, 0], rmv.at[0, 0], ld.at[0]),
        pltpu.make_async_copy(smv.at[1, 0], rmv.at[1, 0], ld.at[2]),
        pltpu.make_async_copy(sw.at[0], rw.at[0], ld.at[1]),
    ]
    for copy in own:
        copy.start()
    tab_o[...] = tab[...]

    for q in ORDER:
        w_copy[q].wait_recv()
    for h in range(2):
        for q in ORDER:
            mv_copy[h, q].wait_recv()
    for copy in own:
        copy.wait()
    for copy in sends:
        copy.wait_send()


def place(tab_s, rw, rmv, ow, om, ov, w_v, mv_v, o_v, w_in, mv_in, w_out, m_out, v_out):
    ins, outs = [], []
    for p in range(ITEMS):
        q = tab_s[0, p]
        ins.append([
            pltpu.make_async_copy(rmv.at[0, q], mv_v.at[:, p, pl.ds(0, H)], mv_in.at[p, 0]),
            pltpu.make_async_copy(rmv.at[1, q], mv_v.at[:, p, pl.ds(H, H)], mv_in.at[p, 1]),
            pltpu.make_async_copy(rw.at[q], w_v.at[p], w_in.at[p]),
        ])
        for copy in ins[p]:
            copy.start()
    for p in range(ITEMS):
        for copy in ins[p]:
            copy.wait()
        first, second, weight = mv_v[0, p], mv_v[1, p], w_v[p]
        first_hat = first / (1.0 - beta_one**STEP)
        second_hat = second / (1.0 - beta_two**STEP)
        o_v[p] = weight - learn_rate * (
            first_hat / (jnp.sqrt(second_hat) + epsilon) + decay_rate * weight
        )
        for src, dst, sem in (
            (mv_v.at[0, p], om.at[p], m_out.at[p]),
            (mv_v.at[1, p], ov.at[p], v_out.at[p]),
            (o_v.at[p], ow.at[p], w_out.at[p]),
        ):
            outs.append(pltpu.make_async_copy(src, dst, sem))
            outs[-1].start()
    for copy in outs:
        copy.wait()


def per_device(
    partial_grads, replica_grads, replica_item, weight, first_moment, second_moment, new_position
):
    f32, i32, bf16 = jnp.float32, jnp.int32, jnp.bfloat16
    vmem, smem, dma = pltpu.VMEM, pltpu.SMEM, pltpu.SemaphoreType.DMA
    slab, half = (R, C), (H, C)
    anywhere = pl.BlockSpec(memory_space=pl.ANY)
    in_smem = pl.BlockSpec(memory_space=pltpu.SMEM)
    in_vmem = pl.BlockSpec(memory_space=pltpu.VMEM)
    rw, rmv, tab = pl.pallas_call(
        kernel,
        out_shape=[
            jax.ShapeDtypeStruct((NE, *slab), f32),
            jax.ShapeDtypeStruct((2, NE, 2, *half), f32),
            jax.ShapeDtypeStruct((8, 128), i32),
        ],
        in_specs=[in_smem, in_smem] + [anywhere] * 5,
        out_specs=[anywhere, anywhere, in_vmem],
        scratch_shapes=[
            vmem((SLABS, R, 8 * C), bf16),
            vmem((ITEMS, *slab), f32),
            vmem((ITEMS, *slab), f32),
            vmem((ITEMS, *slab), f32),
            vmem((SLABS, NX, *slab), f32),
            vmem((SLABS, NX, *slab), f32),
            vmem((SLABS, *slab), f32),
            vmem((2, SLABS, *slab), f32),
            vmem((ITEMS, *slab), f32),
            vmem((2, NY, NZ, 2, *half), f32),
            vmem((2, 2 * NE + 1, *half), f32),
            vmem((NE, *slab), f32),
            vmem((2, NE, 2, *half), f32),
            vmem((8, 128), i32),
            vmem((NY, NZ, 8, 128), i32),
            vmem((8, 128), i32),
            smem((8, 128), i32),
            smem((8, 128), i32),
            dma((12,)),
            dma((2,)),
            dma((len(CHUNKS),)), dma((len(CHUNKS),)),
            dma((len(CHUNKS), 2)), dma((len(CHUNKS), 2)),
            dma((len(CHUNKS), 2)), dma((len(CHUNKS), 2)),
            dma((NZ,)), dma((NZ,)),
            dma((NY,)), dma((NY,)),
            dma((NE,)), dma((NE,)),
            dma((2, NE)), dma((2, NE)),
            dma((2, NZ)), dma((2, NZ)),
            dma((2, len(GROUPS), NY)), dma((2, len(GROUPS), NY)),
        ],
        name="step_and_migrate",
        compiler_params=pltpu.CompilerParams(
            collective_id=0, has_side_effects=True, vmem_limit_bytes=58 << 20
        ),
    )(
        new_position.T,
        replica_item,
        replica_grads[0],
        partial_grads.reshape(ITEMS, R, 8 * C),
        weight.reshape(ITEMS, *slab),
        first_moment.reshape(ITEMS, *slab),
        second_moment.reshape(ITEMS, *slab),
    )
    outs = pl.pallas_call(
        place,
        out_shape=[jax.ShapeDtypeStruct((ITEMS, *slab), f32)] * 3,
        in_specs=[in_smem, anywhere, anywhere],
        out_specs=[anywhere] * 3,
        scratch_shapes=[
            vmem((ITEMS, *slab), f32),
            vmem((2, ITEMS, *slab), f32),
            vmem((ITEMS, *slab), f32),
            dma((ITEMS,)),
            dma((ITEMS, 2)),
        ]
        + [dma((ITEMS,))] * 3,
        name="place",
        compiler_params=pltpu.CompilerParams(vmem_limit_bytes=58 << 20),
    )(tab, rw, rmv)
    return tuple(out.reshape(weight.shape) for out in outs)


def solution(mesh):
    in_specs = (
        P("dp", "expert", None, None, None),
        P("dp", "expert", None, None),
        P("expert"),
        P("expert", None, None, "dp"),
        P("expert", None, None, "dp"),
        P("expert", None, None, "dp"),
        P("expert", None),
    )
    out_specs = (
        P("expert", None, None, "dp"),
        P("expert", None, None, "dp"),
        P("expert", None, None, "dp"),
    )
    return jax.shard_map(
        per_device, mesh=mesh, in_specs=in_specs, out_specs=out_specs, check_vma=False
    )
```
